32 devices in a mesh: row: 16 (over z, y, x), col: 2 (over core).
Axes of the slice: x: 2, y: 2, z: 4, core: 2. Of those that a mesh axis runs over, the one named last changes fastest.
Arguments:
- start_vectors: float32 [8192, 128], P(('row', 'col')), may hold values from -6 to 6
- tiles: bfloat16 [16, 2, 2, 512, 512], P('row', 'col'), may hold values from -0.25 to 0.25
- tile_rows: int32 [16, 2, 2], P('row', 'col'), may hold values from 0 to 0
- tile_cols: int32 [16, 2, 2], P('row', 'col'), may hold values from 0 to 7
- tile_counts: int32 [16, 2], P('row', 'col'), may hold values from 1 to 2, as said below
Outputs:
- basis: float32 [8192, 128], P(('row', 'col'))
- ritz: float32 [128, 128], replicated
The draws below stay inside these ranges and needn't reach their ends.
Inputs may be any that keep to these rules, and one draw needn't show every extreme that they name: Slots 0 to tile_counts - 1 are live, the others are ignored.
All inputs are finite; a program needn't handle non-finite values.
Results may differ from the reference program's by a relative error of at most 0.0047.
The reference program's roundings to bfloat16 on the way count: a program that leaves them out, or rounds other values in their place, can miss the bound.
Values may be sent and summed in bfloat16 or wider, within the bound.
A program may use at most 64 MiB of HBM per device.

```python
import math
import jax
import jax.numpy as jnp
from jax import lax

TILE = 512
KVEC = 128
VR = 256
SLOTS = 2
NVEC = 8192
TR_DEV = 1
TC_DEV = 8
N_ROW = 16
N_COL = 2


def draw_tile_rows(key, part):
    key = jax.random.fold_in(key, 11)
    values = jax.random.randint(key, (N_ROW, N_COL, SLOTS), 0, TR_DEV)
    values = values.at[0, 0, 0].set(TR_DEV - 1)
    values = values.at[0, 0, 1].set(0)
    return values.astype(jnp.int32)


def draw_tile_cols(key, part):
    key = jax.random.fold_in(key, 23)
    values = jax.random.randint(key, (N_ROW, N_COL, SLOTS), 0, TC_DEV)
    values = values.at[0, 0, 0].set(TC_DEV - 1)
    values = values.at[0, 0, 1].set(0)
    return values.astype(jnp.int32)


def draw_tile_counts(key, part):
    key = jax.random.fold_in(key, 37)
    first_key, second_key, third_key, fourth_key = jax.random.split(key, 4)
    first = jax.random.randint(first_key, (N_ROW * N_COL,), 0, SLOTS)
    second = jax.random.randint(second_key, (N_ROW * N_COL,), 0, SLOTS)
    counts = 1 + jnp.minimum(first, second)
    busiest = jax.random.randint(third_key, (), 0, N_ROW * N_COL)
    lightest = (busiest + 1 + jax.random.randint(fourth_key, (), 0, N_ROW * N_COL - 1)) % (N_ROW * N_COL)
    counts = counts.at[busiest].set(SLOTS)
    counts = counts.at[lightest].set(1)
    return counts.reshape(N_ROW, N_COL).astype(jnp.int32)


def block_levels(own_key, shape, cuts, smallest, largest):
    gain = 1.0
    for position, parts in cuts:
        draws = jax.random.uniform(jax.random.fold_in(jax.random.fold_in(own_key, 6), position), (parts,), jnp.float32, smallest / len(cuts), largest / len(cuts))
        gain = gain * jnp.repeat(jnp.exp(draws), shape[position] // parts).reshape((-1,) + (1,) * (len(shape) - 1 - position))
    return gain


def scatter_about(own_key, extent, deviation, most, cuts=(), kind=jnp.bfloat16):
    entries = deviation * jax.random.normal(own_key, extent, jnp.float32)
    if cuts:
        entries = entries * block_levels(own_key, extent, cuts, -0.22, 0.18)
    return jnp.clip(entries, -most, most).astype(kind)


def setup_inputs(seed: int = 0) -> dict:
    splits = jax.random.split(jax.random.key(seed), 6)
    start_vectors = scatter_about(splits[0], (NVEC, KVEC), 1.0, 6.0, ((0, 32),), jnp.float32)
    tiles = scatter_about(splits[1], (N_ROW, N_COL, SLOTS, TILE, TILE), TILE ** -0.5, 0.25, ((0, 16), (1, 2)))
    tile_rows = draw_tile_rows(jax.random.fold_in(splits[5], 71), 0)
    tile_cols = draw_tile_cols(jax.random.fold_in(splits[5], 71), 0)
    tile_counts = draw_tile_counts(jax.random.fold_in(splits[5], 71), 0)
    return dict(start_vectors=start_vectors, tiles=tiles, tile_rows=tile_rows, tile_cols=tile_cols, tile_counts=tile_counts)


def device_term(tile_set, slot_rows, slot_cols, live_count, group):
    picked = group[slot_cols]
    product = jnp.einsum('sij,sjk->sik', tile_set.astype(jnp.float32), picked.astype(jnp.float32))
    slot_ids = jnp.arange(SLOTS).astype(jnp.int32)
    live = slot_ids < live_count
    targets = jnp.arange(TR_DEV).astype(jnp.int32)
    place = ((slot_rows[None, :] == targets[:, None]) & live[None, :]).astype(jnp.float32)
    summed = jnp.einsum('rs,sik->rik', place, product, precision=lax.Precision.HIGHEST)
    return summed.reshape(TR_DEV * TILE, KVEC)

def apply_graph(vectors, tiles, tile_rows, tile_cols, tile_counts):
    rounded = vectors.astype(jnp.bfloat16)
    groups = rounded.reshape(N_ROW, N_COL, VR, KVEC).transpose(1, 0, 2, 3).reshape(N_COL, TC_DEV, TILE, KVEC)

    def block(row_index):

        def add_group(total, col_index):
            term = device_term(tiles[row_index, col_index], tile_rows[row_index, col_index], tile_cols[row_index, col_index], tile_counts[row_index, col_index], groups[col_index])
            return (total + term, None)
        total, _ = lax.scan(add_group, jnp.zeros((TR_DEV * TILE, KVEC), jnp.float32), jnp.arange(N_COL).astype(jnp.int32))
        return total
    blocks = lax.map(block, jnp.arange(N_ROW).astype(jnp.int32))
    return blocks.reshape(NVEC, KVEC)

def normalize(block_rows):
    gram_matrix = jnp.dot(block_rows.T, block_rows, precision=lax.Precision.HIGHEST)
    factor = jnp.linalg.cholesky(gram_matrix)
    solved = lax.linalg.triangular_solve(factor, block_rows, left_side=False, lower=True, transpose_a=True)
    return math.sqrt(NVEC) * solved

def reference(start_vectors, tiles, tile_rows, tile_cols, tile_counts):
    first = apply_graph(start_vectors, tiles, tile_rows, tile_cols, tile_counts)
    middle = normalize(first)
    second = apply_graph(middle, tiles, tile_rows, tile_cols, tile_counts)
    ritz = jnp.dot(middle.T, second, precision=lax.Precision.HIGHEST) / math.sqrt(NVEC)
    basis = normalize(second)
    return (basis, ritz)
```

```python
import functools
import math

import jax
import jax.numpy as jnp
from jax import lax
from jax.experimental import pallas as pl
from jax.experimental.pallas import tpu as pltpu
from jax.sharding import PartitionSpec as P

MESH = pl.DeviceIdType.MESH
HIGHEST = lax.Precision.HIGHEST
PANEL = 16


def dot_tn(left, right):
    return lax.dot_general(
        left, right, (((0,), (0,)), ((), ())), precision=HIGHEST,
        preferred_element_type=jnp.float32,
    )


def dot_nt(left, right):
    return lax.dot_general(
        left, right, (((1,), (1,)), ((), ())), precision=HIGHEST,
        preferred_element_type=jnp.float32,
    )


def invert_factor(gram, work, unit, inverse):
    width = gram.shape[0]
    rows = lax.broadcasted_iota(jnp.int32, (width, width), 0)
    lanes = lax.broadcasted_iota(jnp.int32, (width, width), 1)
    work[...] = gram
    unit[...] = jnp.where(rows == lanes, 1.0, 0.0)
    panel_rows = lax.broadcasted_iota(jnp.int32, (PANEL, width), 0)
    panel_lanes = lax.broadcasted_iota(jnp.int32, (PANEL, width), 1)
    for first in range(0, width, PANEL):
        last = first + PANEL
        left = work[first:last, :]
        right = unit[first:last, :]
        for i in range(PANEL):
            pivot_row = left[i : i + 1, :]
            pivot = pivot_row[:, first + i : first + i + 1]
            factor = left[:, first + i : first + i + 1] * (1.0 / pivot)
            factor = jnp.where(panel_rows > i, factor, 0.0)
            left = left - factor * pivot_row
            right = right - factor * right[i : i + 1, :]
        diagonal = jnp.where(panel_lanes == panel_rows + first, left, 0.0)
        diagonal = jnp.sum(diagonal, axis=1, keepdims=True)
        root = lax.rsqrt(diagonal)
        root = root * (1.5 - 0.5 * ((diagonal * root) * root))
        right = right * root
        inverse[first:last, :] = right
        if last < width:
            left = jnp.where(panel_lanes >= last, left * root, 0.0)
            change = dot_tn(left, left)
            work[last:, :] = work[last:, :] - change[last:, :]
            change = dot_tn(left, right)
            unit[last:, :] = unit[last:, :] - change[last:, :]


def kernel(
    n_row, n_col, inner,
    start_ref, tiles_ref, cols_ref, weights_ref,
    basis_ref, ritz_ref,
    group_first, group_second, parts, landed, grams, gathered, outers, finals, work, unit, inverse,
    near_send, near_recv, far_send, far_recv, part_send, part_recv,
    gram_send, gram_recv, outer_send, outer_recv, final_send, final_recv,
):
    outer = n_row // inner
    members = inner * n_col
    piece, width = start_ref.shape
    slots, tile = tiles_ref.shape[0], tiles_ref.shape[-1]
    chunk = width // members
    scale = math.sqrt(n_row * n_col * piece)
    row = lax.axis_index("row")
    col = lax.axis_index("col")
    out_index = lax.div(row, inner)
    in_index = lax.rem(row, inner)
    member = in_index * n_col + col

    def outer_peer(d):
        return lax.rem(out_index + d + outer, outer)

    def inner_peer(e):
        return lax.rem(in_index + e + inner, inner)

    def member_device(g):
        return (out_index * inner + lax.div(g, n_col), lax.rem(g, n_col))

    def remote(src, dst, send, recv, device):
        return pltpu.make_async_remote_copy(
            src_ref=src, dst_ref=dst, send_sem=send, recv_sem=recv,
            device_id=device, device_id_type=MESH,
        )

    barrier = pltpu.get_barrier_semaphore()
    for d in range(1, outer):
        pl.semaphore_signal(
            barrier, inc=1, device_id=(outer_peer(d) * inner + in_index, col),
            device_id_type=MESH,
        )
    for e in range(1, members):
        pl.semaphore_signal(
            barrier, inc=1, device_id=member_device(lax.rem(member + e, members)),
            device_id_type=MESH,
        )
    pl.semaphore_wait(barrier, outer - 1 + members - 1)

    def block_at(step, index):
        group = (group_first, group_second)[step]
        at = index * piece
        return group.at[lax.div(at, tile), pl.ds(pl.multiple_of(lax.rem(at, tile), piece), piece)]

    vectors = start_ref[...]
    for step in range(2):
        started = []
        total = step + 1

        def send(copy):
            copy.start()
            started.append(copy)

        own = block_at(step, row)
        own[...] = vectors.astype(jnp.bfloat16)
        for d in range(1, outer):
            send(remote(own, own, far_send.at[d], far_recv.at[d],
                        (outer_peer(d) * inner + in_index, col)))
        for d in range(outer):
            held = block_at(step, outer_peer(-d) * inner + in_index)
            if d > 0:
                remote(held, held, far_send.at[d], far_recv.at[d],
                       (outer_peer(-d) * inner + in_index, col)).wait_recv()
            for e in range(1, inner):
                send(remote(held, held, near_send.at[d * inner + e], near_recv.at[d * inner + e],
                            (out_index * inner + inner_peer(e), col)))
        for d in range(outer):
            for e in range(1, inner):
                came = block_at(step, outer_peer(-d) * inner + inner_peer(-e))
                remote(came, came, near_send.at[d * inner + e], near_recv.at[d * inner + e],
                       (out_index * inner + inner_peer(-e), col)).wait_recv()

        group = (group_first, group_second)[step]
        picked = [group[cols_ref[0, 0, s]] for s in range(slots)]
        for k in list(range(1, n_col)) + [0]:
            owner = lax.rem(col + k, n_col)
            at = owner * piece
            tile_row = lax.div(at, tile)
            offset = pl.multiple_of(lax.rem(at, tile), piece)
            value = jnp.zeros((piece, width), jnp.float32)
            for s in range(slots):
                product = jnp.dot(
                    tiles_ref[s, pl.ds(offset, piece), :], picked[s],
                    preferred_element_type=jnp.float32,
                )
                value = value + weights_ref[s, tile_row] * product
            if k > 0:
                parts[step, k] = value
                send(remote(parts.at[step, k], landed.at[step, col], part_send.at[k],
                            part_recv.at[k], (row, owner)))
            else:
                landed[step, col] = value
        for k in range(1, n_col):
            source = lax.rem(col - k + n_col, n_col)
            remote(parts.at[step, k], landed.at[step, source], part_send.at[k],
                   part_recv.at[k], (row, source)).wait_recv()
        mine = landed[step, 0]
        for c in range(1, n_col):
            mine = mine + landed[step, c]

        mats = [dot_tn(mine, mine)]
        if step == 1:
            mats.append(dot_tn(vectors, mine))
        for g in range(members):
            for m in range(total):
                grams[step, g, m * chunk : (m + 1) * chunk, :] = mats[m][g * chunk : (g + 1) * chunk, :]
        used_rows = pl.ds(0, total * chunk)
        for e in range(1, members):
            target = lax.rem(member + e, members)
            send(remote(grams.at[step, target, used_rows], gathered.at[step, e, used_rows],
                        gram_send.at[e], gram_recv.at[e], member_device(target)))
        sums = grams[step, member, 0 : total * chunk, :]
        for e in range(1, members):
            source = lax.rem(member - e + members, members)
            slot = gathered.at[step, e, used_rows]
            remote(slot, slot, gram_send.at[e], gram_recv.at[e], member_device(source)).wait_recv()
            sums = sums + gathered[step, e, 0 : total * chunk, :]
        own = outers.at[step, out_index, used_rows]
        own[...] = sums
        for d in range(1, outer):
            send(remote(own, own, outer_send.at[d], outer_recv.at[d],
                        (outer_peer(d) * inner + in_index, col)))
        for d in range(1, outer):
            came = outers.at[step, outer_peer(-d), used_rows]
            remote(came, came, outer_send.at[d], outer_recv.at[d],
                   (outer_peer(-d) * inner + in_index, col)).wait_recv()
        sums = outers[step, 0, 0 : total * chunk, :]
        for d in range(1, outer):
            sums = sums + outers[step, d, 0 : total * chunk, :]
        own = finals.at[step, member, used_rows]
        own[...] = sums
        for e in range(1, members):
            send(remote(own, own, final_send.at[e], final_recv.at[e],
                        member_device(lax.rem(member + e, members))))
        for e in range(1, members):
            source = lax.rem(member - e + members, members)
            came = finals.at[step, source, used_rows]
            remote(came, came, final_send.at[e], final_recv.at[e], member_device(source)).wait_recv()
        gram = jnp.concatenate([finals[step, g, 0:chunk, :] for g in range(members)], axis=0)
        if step == 1:
            for g in range(members):
                ritz_ref[g * chunk : (g + 1) * chunk, :] = finals[step, g, chunk : 2 * chunk, :] / scale

        invert_factor(gram, work, unit, inverse)
        vectors = scale * dot_nt(mine, inverse[...])
        for copy in started:
            copy.wait_send()
    basis_ref[...] = vectors


def per_device(n_row, n_col, start_vectors, tiles, tile_rows, tile_cols, tile_counts):
    piece, width = start_vectors.shape
    slots, tile = tiles.shape[2], tiles.shape[-1]
    targets = jnp.arange(n_col * piece // tile, dtype=jnp.int32)
    live = jnp.arange(slots, dtype=jnp.int32) < tile_counts[0, 0]
    placed = tile_rows[0, 0][:, None] == targets[None, :]
    weights = jnp.logical_and(placed, live[:, None]).astype(jnp.float32)
    inner = max(1, 8 // n_col)
    outer = n_row // inner
    members = inner * n_col
    chunk = width // members
    f32 = jnp.float32
    vmem = pl.BlockSpec(memory_space=pltpu.VMEM)
    smem = pl.BlockSpec(memory_space=pltpu.SMEM)
    dma = pltpu.SemaphoreType.DMA
    pairs = []
    for count in (outer * inner, outer, n_col, members, outer, members):
        pairs += [dma((count,)), dma((count,))]
    return pl.pallas_call(
        functools.partial(kernel, n_row, n_col, inner),
        out_shape=(
            jax.ShapeDtypeStruct((piece, width), f32),
            jax.ShapeDtypeStruct((width, width), f32),
        ),
        in_specs=[vmem, vmem, smem, smem],
        out_specs=(vmem, vmem),
        scratch_shapes=[
            pltpu.VMEM((n_row * piece // tile, tile, width), jnp.bfloat16),
            pltpu.VMEM((n_row * piece // tile, tile, width), jnp.bfloat16),
            pltpu.VMEM((2, n_col, piece, width), f32),
            pltpu.VMEM((2, n_col, piece, width), f32),
            pltpu.VMEM((2, members, 2 * chunk, width), f32),
            pltpu.VMEM((2, members, 2 * chunk, width), f32),
            pltpu.VMEM((2, outer, 2 * chunk, width), f32),
            pltpu.VMEM((2, members, 2 * chunk, width), f32),
            pltpu.VMEM((width, width), f32),
            pltpu.VMEM((width, width), f32),
            pltpu.VMEM((width, width), f32),
        ] + pairs,
        compiler_params=pltpu.CompilerParams(
            collective_id=0, has_side_effects=True, vmem_limit_bytes=40 * 1024 * 1024,
        ),
        name="krylov",
    )(start_vectors, tiles[0, 0], tile_cols, weights)


def solution(mesh):
    placed = (
        P(("row", "col"), None),
        P("row", "col", None, None, None),
        P("row", "col", None),
        P("row", "col", None),
        P("row", "col"),
    )
    return jax.shard_map(
        functools.partial(per_device, mesh.shape["row"], mesh.shape["col"]),
        mesh=mesh,
        in_specs=placed,
        out_specs=(P(("row", "col"), None), P()),
        check_vma=False,
    )
```

```python
import functools
import math

import jax
import jax.numpy as jnp
from jax import lax
from jax.experimental import pallas as pl
from jax.experimental.pallas import tpu as pltpu
from jax.sharding import PartitionSpec as P

MESH = pl.DeviceIdType.MESH
HIGHEST = lax.Precision.HIGHEST
PANEL = 16


def dot_tn(left, right):
    return lax.dot_general(
        left, right, (((0,), (0,)), ((), ())), precision=HIGHEST,
        preferred_element_type=jnp.float32,
    )


def dot_nt(left, right):
    return lax.dot_general(
        left, right, (((1,), (1,)), ((), ())), precision=HIGHEST,
        preferred_element_type=jnp.float32,
    )


def invert_factor(gram, work, unit, inverse):
    width = gram.shape[0]
    rows = lax.broadcasted_iota(jnp.int32, (width, width), 0)
    lanes = lax.broadcasted_iota(jnp.int32, (width, width), 1)
    work[...] = gram
    unit[...] = jnp.where(rows == lanes, 1.0, 0.0)
    panel_rows = lax.broadcasted_iota(jnp.int32, (PANEL, width), 0)
    panel_lanes = lax.broadcasted_iota(jnp.int32, (PANEL, width), 1)
    for first in range(0, width, PANEL):
        last = first + PANEL
        left = work[first:last, :]
        right = unit[first:last, :]
        spread = [
            jnp.broadcast_to(left[:, first + k : first + k + 1], (PANEL, width))
            for k in range(PANEL)
        ]
        diagonal = spread[0]
        for i in range(PANEL):
            column = spread[i]
            if i > 0:
                diagonal = jnp.where(panel_rows == i, column, diagonal)
            if i == PANEL - 1:
                break
            factor = jnp.where(panel_rows > i, column * (1.0 / column[i : i + 1, :]), 0.0)
            for k in range(i + 1, PANEL):
                spread[k] = spread[k] - factor * spread[k][i : i + 1, :]
            left = left - factor * left[i : i + 1, :]
            right = right - factor * right[i : i + 1, :]
        root = lax.rsqrt(diagonal)
        root = root * (1.5 - 0.5 * ((diagonal * root) * root))
        right = right * root
        inverse[first:last, :] = right
        if last < width:
            left = jnp.where(panel_lanes >= last, left * root, 0.0)
            change = dot_tn(left, left)
            work[last:, :] = work[last:, :] - change[last:, :]
            change = dot_tn(left, right)
            unit[last:, :] = unit[last:, :] - change[last:, :]


def kernel(
    n_row, n_col, inner,
    start_ref, tiles_hbm, cols_ref, weights_ref,
    basis_ref, ritz_ref,
    group_first, group_second, parts, landed, grams, gathered, outers, finals, work, unit, inverse,
    tiles_ref, tiles_sem,
    near_send, near_recv, far_send, far_recv, part_send, part_recv,
    gram_send, gram_recv, outer_send, outer_recv, final_send, final_recv,
):
    outer = n_row // inner
    members = inner * n_col
    piece, width = start_ref.shape
    slots, tile = tiles_ref.shape[0], tiles_ref.shape[-1]
    chunk = width // members
    scale = math.sqrt(n_row * n_col * piece)
    row = lax.axis_index("row")
    col = lax.axis_index("col")
    out_index = lax.div(row, inner)
    in_index = lax.rem(row, inner)
    member = in_index * n_col + col

    def outer_peer(d):
        return lax.rem(out_index + d + outer, outer)

    def inner_peer(e):
        return lax.rem(in_index + e + inner, inner)

    def member_device(g):
        return (out_index * inner + lax.div(g, n_col), lax.rem(g, n_col))

    def remote(src, dst, send, recv, device):
        return pltpu.make_async_remote_copy(
            src_ref=src, dst_ref=dst, send_sem=send, recv_sem=recv,
            device_id=device, device_id_type=MESH,
        )

    loading = pltpu.make_async_copy(tiles_hbm, tiles_ref, tiles_sem)
    loading.start()
    barrier = pltpu.get_barrier_semaphore()
    for d in range(1, outer):
        pl.semaphore_signal(
            barrier, inc=1, device_id=(outer_peer(d) * inner + in_index, col),
            device_id_type=MESH,
        )
    for e in range(1, members):
        pl.semaphore_signal(
            barrier, inc=1, device_id=member_device(lax.rem(member + e, members)),
            device_id_type=MESH,
        )
    pl.semaphore_wait(barrier, outer - 1 + members - 1)

    def block_at(step, index):
        group = (group_first, group_second)[step]
        at = index * piece
        return group.at[lax.div(at, tile), pl.ds(pl.multiple_of(lax.rem(at, tile), piece), piece)]

    vectors = start_ref[...]
    for step in range(2):
        started = []
        total = step + 1

        def send(copy):
            copy.start()
            started.append(copy)

        own = block_at(step, row)
        own[...] = vectors.astype(jnp.bfloat16)
        for d in range(1, outer):
            send(remote(own, own, far_send.at[d], far_recv.at[d],
                        (outer_peer(d) * inner + in_index, col)))
        for d in range(outer):
            held = block_at(step, outer_peer(-d) * inner + in_index)
            if d > 0:
                remote(held, held, far_send.at[d], far_recv.at[d],
                       (outer_peer(-d) * inner + in_index, col)).wait_recv()
            for e in range(1, inner):
                send(remote(held, held, near_send.at[d * inner + e], near_recv.at[d * inner + e],
                            (out_index * inner + inner_peer(e), col)))
        for d in range(outer):
            for e in range(1, inner):
                came = block_at(step, outer_peer(-d) * inner + inner_peer(-e))
                remote(came, came, near_send.at[d * inner + e], near_recv.at[d * inner + e],
                       (out_index * inner + inner_peer(-e), col)).wait_recv()

        group = (group_first, group_second)[step]
        if step == 0:
            loading.wait()
        picked = [group[cols_ref[0, 0, s]] for s in range(slots)]
        for k in list(range(1, n_col)) + [0]:
            owner = lax.rem(col + k, n_col)
            at = owner * piece
            tile_row = lax.div(at, tile)
            offset = pl.multiple_of(lax.rem(at, tile), piece)
            value = jnp.zeros((piece, width), jnp.float32)
            for s in range(slots):
                product = jnp.dot(
                    tiles_ref[s, pl.ds(offset, piece), :], picked[s],
                    preferred_element_type=jnp.float32,
                )
                value = value + weights_ref[s, tile_row] * product
            if k > 0:
                parts[step, k] = value
                send(remote(parts.at[step, k], landed.at[step, col], part_send.at[k],
                            part_recv.at[k], (row, owner)))
            else:
                landed[step, col] = value
        for k in range(1, n_col):
            source = lax.rem(col - k + n_col, n_col)
            remote(parts.at[step, k], landed.at[step, source], part_send.at[k],
                   part_recv.at[k], (row, source)).wait_recv()
        mine = landed[step, 0]
        for c in range(1, n_col):
            mine = mine + landed[step, c]

        mats = [dot_tn(mine, mine)]
        if step == 1:
            mats.append(dot_tn(vectors, mine))
        for g in range(members):
            for m in range(total):
                grams[step, g, m * chunk : (m + 1) * chunk, :] = mats[m][g * chunk : (g + 1) * chunk, :]
        used_rows = pl.ds(0, total * chunk)
        for e in range(1, members):
            target = lax.rem(member + e, members)
            send(remote(grams.at[step, target, used_rows], gathered.at[step, e, used_rows],
                        gram_send.at[e], gram_recv.at[e], member_device(target)))
        sums = grams[step, member, 0 : total * chunk, :]
        for e in range(1, members):
            source = lax.rem(member - e + members, members)
            slot = gathered.at[step, e, used_rows]
            remote(slot, slot, gram_send.at[e], gram_recv.at[e], member_device(source)).wait_recv()
            sums = sums + gathered[step, e, 0 : total * chunk, :]
        own = outers.at[step, out_index, used_rows]
        own[...] = sums
        for d in range(1, outer):
            send(remote(own, own, outer_send.at[d], outer_recv.at[d],
                        (outer_peer(d) * inner + in_index, col)))
        for d in range(1, outer):
            came = outers.at[step, outer_peer(-d), used_rows]
            remote(came, came, outer_send.at[d], outer_recv.at[d],
                   (outer_peer(-d) * inner + in_index, col)).wait_recv()
        sums = outers[step, 0, 0 : total * chunk, :]
        for d in range(1, outer):
            sums = sums + outers[step, d, 0 : total * chunk, :]
        own = finals.at[step, member, used_rows]
        own[...] = sums
        for e in range(1, members):
            send(remote(own, own, final_send.at[e], final_recv.at[e],
                        member_device(lax.rem(member + e, members))))
        for e in range(1, members):
            source = lax.rem(member - e + members, members)
            came = finals.at[step, source, used_rows]
            remote(came, came, final_send.at[e], final_recv.at[e], member_device(source)).wait_recv()
        gram = jnp.concatenate([finals[step, g, 0:chunk, :] for g in range(members)], axis=0)
        if step == 1:
            for g in range(members):
                ritz_ref[g * chunk : (g + 1) * chunk, :] = finals[step, g, chunk : 2 * chunk, :] / scale

        invert_factor(gram, work, unit, inverse)
        vectors = scale * dot_nt(mine, inverse[...])
        for copy in started:
            copy.wait_send()
    basis_ref[...] = vectors


def per_device(n_row, n_col, start_vectors, tiles, tile_rows, tile_cols, tile_counts):
    piece, width = start_vectors.shape
    slots, tile = tiles.shape[2], tiles.shape[-1]
    targets = jnp.arange(n_col * piece // tile, dtype=jnp.int32)
    live = jnp.arange(slots, dtype=jnp.int32) < tile_counts[0, 0]
    placed = tile_rows[0, 0][:, None] == targets[None, :]
    weights = jnp.logical_and(placed, live[:, None]).astype(jnp.float32)
    inner = max(1, 8 // n_col)
    outer = n_row // inner
    members = inner * n_col
    chunk = width // members
    f32 = jnp.float32
    vmem = pl.BlockSpec(memory_space=pltpu.VMEM)
    smem = pl.BlockSpec(memory_space=pltpu.SMEM)
    dma = pltpu.SemaphoreType.DMA
    pairs = []
    for count in (outer * inner, outer, n_col, members, outer, members):
        pairs += [dma((count,)), dma((count,))]
    return pl.pallas_call(
        functools.partial(kernel, n_row, n_col, inner),
        out_shape=(
            jax.ShapeDtypeStruct((piece, width), f32),
            jax.ShapeDtypeStruct((width, width), f32),
        ),
        in_specs=[vmem, pl.BlockSpec(memory_space=pl.ANY), smem, smem],
        out_specs=(vmem, vmem),
        scratch_shapes=[
            pltpu.VMEM((n_row * piece // tile, tile, width), jnp.bfloat16),
            pltpu.VMEM((n_row * piece // tile, tile, width), jnp.bfloat16),
            pltpu.VMEM((2, n_col, piece, width), f32),
            pltpu.VMEM((2, n_col, piece, width), f32),
            pltpu.VMEM((2, members, 2 * chunk, width), f32),
            pltpu.VMEM((2, members, 2 * chunk, width), f32),
            pltpu.VMEM((2, outer, 2 * chunk, width), f32),
            pltpu.VMEM((2, members, 2 * chunk, width), f32),
            pltpu.VMEM((width, width), f32),
            pltpu.VMEM((width, width), f32),
            pltpu.VMEM((width, width), f32),
            pltpu.VMEM(tiles.shape[2:], tiles.dtype),
            dma(()),
        ] + pairs,
        compiler_params=pltpu.CompilerParams(
            collective_id=0, has_side_effects=True, vmem_limit_bytes=40 * 1024 * 1024,
        ),
        name="krylov",
    )(start_vectors, tiles[0, 0], tile_cols, weights)


def solution(mesh):
    placed = (
        P(("row", "col"), None),
        P("row", "col", None, None, None),
        P("row", "col", None),
        P("row", "col", None),
        P("row", "col"),
    )
    return jax.shard_map(
        functools.partial(per_device, mesh.shape["row"], mesh.shape["col"]),
        mesh=mesh,
        in_specs=placed,
        out_specs=(P(("row", "col"), None), P()),
        check_vma=False,
    )
```

```python
import functools
import math

import jax
import jax.numpy as jnp
from jax import lax
from jax.experimental import pallas as pl
from jax.experimental.pallas import tpu as pltpu
from jax.sharding import PartitionSpec as P

MESH = pl.DeviceIdType.MESH
HIGHEST = lax.Precision.HIGHEST
PANEL = 32


def dot_tn(left, right):
    return lax.dot_general(
        left, right, (((0,), (0,)), ((), ())), precision=HIGHEST,
        preferred_element_type=jnp.float32,
    )


def dot_nt(left, right):
    return lax.dot_general(
        left, right, (((1,), (1,)), ((), ())), precision=HIGHEST,
        preferred_element_type=jnp.float32,
    )


def invert_factor(gram, work, unit, inverse):
    width = gram.shape[0]
    rows = lax.broadcasted_iota(jnp.int32, (width, width), 0)
    lanes = lax.broadcasted_iota(jnp.int32, (width, width), 1)
    work[...] = gram
    unit[...] = jnp.where(rows == lanes, 1.0, 0.0)
    panel_rows = lax.broadcasted_iota(jnp.int32, (PANEL, width), 0)
    panel_lanes = lax.broadcasted_iota(jnp.int32, (PANEL, width), 1)
    for first in range(0, width, PANEL):
        last = first + PANEL
        left = work[first:last, :]
        right = unit[first:last, :]
        spread = [
            jnp.broadcast_to(left[:, first + k : first + k + 1], (PANEL, width))
            for k in range(PANEL)
        ]
        diagonal = spread[0]
        for i in range(PANEL):
            column = spread[i]
            if i > 0:
                diagonal = jnp.where(panel_rows == i, column, diagonal)
            if i == PANEL - 1:
                break
            factor = jnp.where(panel_rows > i, column * (1.0 / column[i : i + 1, :]), 0.0)
            for k in range(i + 1, PANEL):
                spread[k] = spread[k] - factor * spread[k][i : i + 1, :]
            left = left - factor * left[i : i + 1, :]
            right = right - factor * right[i : i + 1, :]
        root = lax.rsqrt(diagonal)
        root = root * (1.5 - 0.5 * ((diagonal * root) * root))
        right = right * root
        inverse[first:last, :] = right
        if last < width:
            left = jnp.where(panel_lanes >= last, left * root, 0.0)
            change = dot_tn(left, left)
            work[last:, :] = work[last:, :] - change[last:, :]
            change = dot_tn(left, right)
            unit[last:, :] = unit[last:, :] - change[last:, :]


def kernel(
    n_row, n_col, inner,
    start_hbm, tiles_hbm, rows_ref, cols_ref, counts_ref,
    basis_ref, ritz_ref,
    group_first, group_second, parts, landed, grams, gathered, outers, finals, work, unit, inverse,
    tiles_ref, start_ref, tiles_sem, start_sem,
    near_send, near_recv, far_send, far_recv, part_send, part_recv,
    gram_send, gram_recv, outer_send, outer_recv, final_send, final_recv,
):
    outer = n_row // inner
    members = inner * n_col
    piece, width = start_ref.shape
    slots, tile = tiles_ref.shape[0], tiles_ref.shape[-1]
    chunk = width // members
    scale = math.sqrt(n_row * n_col * piece)
    row = lax.axis_index("row")
    col = lax.axis_index("col")
    out_index = lax.div(row, inner)
    in_index = lax.rem(row, inner)
    member = in_index * n_col + col

    def outer_peer(d):
        return lax.rem(out_index + d + outer, outer)

    def inner_peer(e):
        return lax.rem(in_index + e + inner, inner)

    def member_device(g):
        return (out_index * inner + lax.div(g, n_col), lax.rem(g, n_col))

    def remote(src, dst, send, recv, device):
        return pltpu.make_async_remote_copy(
            src_ref=src, dst_ref=dst, send_sem=send, recv_sem=recv,
            device_id=device, device_id_type=MESH,
        )

    loading = pltpu.make_async_copy(tiles_hbm, tiles_ref, tiles_sem)
    starting = pltpu.make_async_copy(start_hbm, start_ref, start_sem)
    starting.start()
    loading.start()
    barrier = pltpu.get_barrier_semaphore()
    for d in range(1, outer):
        pl.semaphore_signal(
            barrier, inc=1, device_id=(outer_peer(d) * inner + in_index, col),
            device_id_type=MESH,
        )
    for e in range(1, members):
        pl.semaphore_signal(
            barrier, inc=1, device_id=member_device(lax.rem(member + e, members)),
            device_id_type=MESH,
        )
    pl.semaphore_wait(barrier, outer - 1 + members - 1)

    def block_at(step, index):
        group = (group_first, group_second)[step]
        at = index * piece
        return group.at[lax.div(at, tile), pl.ds(pl.multiple_of(lax.rem(at, tile), piece), piece)]

    starting.wait()
    vectors = start_ref[...]
    for step in range(2):
        started = []
        total = step + 1

        def send(copy):
            copy.start()
            started.append(copy)

        own = block_at(step, row)
        own[...] = vectors.astype(jnp.bfloat16)
        for d in range(1, outer):
            send(remote(own, own, far_send.at[d], far_recv.at[d],
                        (outer_peer(d) * inner + in_index, col)))
        for d in range(outer):
            held = block_at(step, outer_peer(-d) * inner + in_index)
            if d > 0:
                remote(held, held, far_send.at[d], far_recv.at[d],
                       (outer_peer(-d) * inner + in_index, col)).wait_recv()
            for e in range(1, inner):
                send(remote(held, held, near_send.at[d * inner + e], near_recv.at[d * inner + e],
                            (out_index * inner + inner_peer(e), col)))
        for d in range(outer):
            for e in range(1, inner):
                came = block_at(step, outer_peer(-d) * inner + inner_peer(-e))
                remote(came, came, near_send.at[d * inner + e], near_recv.at[d * inner + e],
                       (out_index * inner + inner_peer(-e), col)).wait_recv()

        group = (group_first, group_second)[step]
        if step == 0:
            loading.wait()
        picked = [group[cols_ref[0, 0, s]] for s in range(slots)]
        for k in list(range(1, n_col)) + [0]:
            owner = lax.rem(col + k, n_col)
            at = owner * piece
            tile_row = lax.div(at, tile)
            offset = pl.multiple_of(lax.rem(at, tile), piece)
            value = jnp.zeros((piece, width), jnp.float32)
            for s in range(slots):
                apart = rows_ref[0, 0, s] - tile_row
                weight = jnp.maximum(1 - apart * apart, 0) * jnp.minimum(jnp.maximum(counts_ref[0, 0] - s, 0), 1)
                product = jnp.dot(
                    tiles_ref[s, pl.ds(offset, piece), :], picked[s],
                    preferred_element_type=jnp.float32,
                )
                value = value + weight.astype(jnp.float32) * product
            if k > 0:
                parts[step, k] = value
                send(remote(parts.at[step, k], landed.at[step, col], part_send.at[k],
                            part_recv.at[k], (row, owner)))
            else:
                landed[step, col] = value
        for k in range(1, n_col):
            source = lax.rem(col - k + n_col, n_col)
            remote(parts.at[step, k], landed.at[step, source], part_send.at[k],
                   part_recv.at[k], (row, source)).wait_recv()
        mine = landed[step, 0]
        for c in range(1, n_col):
            mine = mine + landed[step, c]

        mats = [dot_tn(mine, mine)]
        if step == 1:
            mats.append(dot_tn(vectors, mine))
        for g in range(members):
            for m in range(total):
                grams[step, g, m * chunk : (m + 1) * chunk, :] = mats[m][g * chunk : (g + 1) * chunk, :]
        used_rows = pl.ds(0, total * chunk)
        for e in range(1, members):
            target = lax.rem(member + e, members)
            send(remote(grams.at[step, target, used_rows], gathered.at[step, e, used_rows],
                        gram_send.at[e], gram_recv.at[e], member_device(target)))
        sums = grams[step, member, 0 : total * chunk, :]
        for e in range(1, members):
            source = lax.rem(member - e + members, members)
            slot = gathered.at[step, e, used_rows]
            remote(slot, slot, gram_send.at[e], gram_recv.at[e], member_device(source)).wait_recv()
            sums = sums + gathered[step, e, 0 : total * chunk, :]
        own = outers.at[step, out_index, used_rows]
        own[...] = sums
        for d in range(1, outer):
            send(remote(own, own, outer_send.at[d], outer_recv.at[d],
                        (outer_peer(d) * inner + in_index, col)))
        for d in range(1, outer):
            came = outers.at[step, outer_peer(-d), used_rows]
            remote(came, came, outer_send.at[d], outer_recv.at[d],
                   (outer_peer(-d) * inner + in_index, col)).wait_recv()
        sums = outers[step, 0, 0 : total * chunk, :]
        for d in range(1, outer):
            sums = sums + outers[step, d, 0 : total * chunk, :]
        own = finals.at[step, member, used_rows]
        own[...] = sums
        for e in range(1, members):
            send(remote(own, own, final_send.at[e], final_recv.at[e],
                        member_device(lax.rem(member + e, members))))
        for e in range(1, members):
            source = lax.rem(member - e + members, members)
            came = finals.at[step, source, used_rows]
            remote(came, came, final_send.at[e], final_recv.at[e], member_device(source)).wait_recv()
        gram = jnp.concatenate([finals[step, g, 0:chunk, :] for g in range(members)], axis=0)
        if step == 1:
            for g in range(members):
                ritz_ref[g * chunk : (g + 1) * chunk, :] = finals[step, g, chunk : 2 * chunk, :] / scale

        invert_factor(gram, work, unit, inverse)
        vectors = scale * dot_nt(mine, inverse[...])
        for copy in started:
            copy.wait_send()
    basis_ref[...] = vectors


def per_device(n_row, n_col, start_vectors, tiles, tile_rows, tile_cols, tile_counts):
    piece, width = start_vectors.shape
    tile = tiles.shape[-1]
    inner = max(1, 8 // n_col)
    outer = n_row // inner
    members = inner * n_col
    chunk = width // members
    f32 = jnp.float32
    vmem = pl.BlockSpec(memory_space=pltpu.VMEM)
    hbm = pl.BlockSpec(memory_space=pl.ANY)
    smem = pl.BlockSpec(memory_space=pltpu.SMEM)
    dma = pltpu.SemaphoreType.DMA
    pairs = []
    for count in (outer * inner, outer, n_col, members, outer, members):
        pairs += [dma((count,)), dma((count,))]
    return pl.pallas_call(
        functools.partial(kernel, n_row, n_col, inner),
        out_shape=(
            jax.ShapeDtypeStruct((piece, width), f32),
            jax.ShapeDtypeStruct((width, width), f32),
        ),
        in_specs=[hbm, hbm, smem, smem, smem],
        out_specs=(vmem, vmem),
        scratch_shapes=[
            pltpu.VMEM((n_row * piece // tile, tile, width), jnp.bfloat16),
            pltpu.VMEM((n_row * piece // tile, tile, width), jnp.bfloat16),
            pltpu.VMEM((2, n_col, piece, width), f32),
            pltpu.VMEM((2, n_col, piece, width), f32),
            pltpu.VMEM((2, members, 2 * chunk, width), f32),
            pltpu.VMEM((2, members, 2 * chunk, width), f32),
            pltpu.VMEM((2, outer, 2 * chunk, width), f32),
            pltpu.VMEM((2, members, 2 * chunk, width), f32),
            pltpu.VMEM((width, width), f32),
            pltpu.VMEM((width, width), f32),
            pltpu.VMEM((width, width), f32),
            pltpu.VMEM(tiles.shape[2:], tiles.dtype),
            pltpu.VMEM((piece, width), f32),
            dma(()),
            dma(()),
        ] + pairs,
        compiler_params=pltpu.CompilerParams(
            collective_id=0, has_side_effects=True, vmem_limit_bytes=60 * 1024 * 1024,
        ),
        name="krylov",
    )(start_vectors, tiles[0, 0], tile_rows, tile_cols, tile_counts)


def solution(mesh):
    placed = (
        P(("row", "col"), None),
        P("row", "col", None, None, None),
        P("row", "col", None),
        P("row", "col", None),
        P("row", "col"),
    )
    return jax.shard_map(
        functools.partial(per_device, mesh.shape["row"], mesh.shape["col"]),
        mesh=mesh,
        in_specs=placed,
        out_specs=(P(("row", "col"), None), P()),
        check_vma=False,
    )
```
